1024 devices in a mesh: dp: 64 (over z_lo, x, core), mp: 16 (over y, z_hi).
Axes of the slice: x: 8, y: 8, z: 8 (z_hi: 2, z_lo: 4; z = z_hi * 4 + z_lo), core: 2. Of those that a mesh axis runs over, the one named last changes fastest.
Arguments:
- patches: bfloat16 [8192, 3072], P('dp', 'mp'), may hold values from -16 to 16
- pre_act: bfloat16 [8192, 12288], P('dp', 'mp'), may hold values from -6 to 6
- cotangent: bfloat16 [8192, 3072], P('dp', 'mp'), may hold values from -16 to 16
- w_up: bfloat16 [3072, 12288], P(None, 'mp'), may hold values from -0.109375 to 0.109375
- w_down: bfloat16 [12288, 3072], P('mp'), may hold values from -0.0546875 to 0.0546875
Outputs:
- grad_patches: bfloat16 [8192, 3072], P('dp', 'mp')
- grad_up: float32 [3072, 12288], P('dp', 'mp')
The draws below stay inside these ranges and needn't reach their ends.
All inputs are finite; a program needn't handle non-finite values.
Results may differ from the reference program's by a relative error of at most 0.013.
Values may be sent and summed in bfloat16 or wider, within the bound.
A program may use at most 64 MiB of HBM per device.

```python
import math
import jax
import jax.numpy as jnp
from jax import lax

D = 3072
FF_DEV = 768
TOKENS = 8192
FF = 12288
N_MP = 16


def strengthened(array, own_key, source, target, shards_of, factor):
    owner, partner = [(jnp.arange(array.shape[dim]) // (array.shape[dim] // shards_of)).reshape([-1 if axis == dim else 1 for axis in range(array.ndim)]) for dim in (source, target)]
    chosen = jax.random.permutation(own_key, shards_of)[partner]
    strong = (owner == chosen) | (owner == (partner + shards_of // 2) % shards_of)
    return jnp.where(strong, factor * array, array)


def level_of(own_key, dims, cuts, least, high):
    loudness = 1.0
    for dim, parts in cuts:
        steps = jax.random.uniform(jax.random.fold_in(jax.random.fold_in(own_key, 6), dim), (parts,), jnp.float32, least / len(cuts), high / len(cuts))
        loudness = loudness * jnp.repeat(jnp.exp(steps), dims[dim] // parts).reshape((-1,) + (1,) * (len(dims) - 1 - dim))
    return loudness


def normal_values(stream_key, shape, deviation, bound, pieces=(), dtype=jnp.bfloat16):
    entries = jax.random.normal(stream_key, shape, jnp.float32) * deviation
    if len(pieces) > 0:
        entries = level_of(stream_key, shape, pieces, -0.22, 0.18) * entries
    return jnp.clip(entries, min=-bound, max=bound).astype(dtype)


def bell_draw_with(key, extent, scale, reach, cuts, heavy, kind=jnp.bfloat16):
    entries = scale * jax.random.normal(key, extent, jnp.float32)
    if cuts:
        entries = entries * level_of(key, extent, cuts, -0.22, 0.18)
    return jnp.clip(strengthened(entries, jax.random.fold_in(key, 3), *heavy), -reach, reach).astype(kind)


def setup_inputs(seed: int = 0) -> dict:
    seeds = jax.random.split(jax.random.key(seed), 6)
    patches = bell_draw_with(seeds[0], (TOKENS, D), 1.0, 16.0, ((0, 64), (1, 16)), (0, 1, 64, 4.0))
    pre_act = normal_values(seeds[1], (TOKENS, FF), 1.0, 6.0, ((0, 64), (1, 16)))
    cotangent = bell_draw_with(seeds[2], (TOKENS, D), 1.0, 16.0, ((0, 64), (1, 16)), (0, 1, 64, 4.0))
    w_up = normal_values(seeds[3], (D, FF), D ** -0.5, 0.109375, ((1, 16),))
    w_down = normal_values(seeds[4], (FF, D), FF ** -0.5, 0.0546875, ((0, 16),))
    return {"patches": patches, "pre_act": pre_act, "cotangent": cotangent, "w_up": w_up, "w_down": w_down}


def gelu_slope(value):
    cdf_part = 0.5 * (1.0 + lax.erf(value * (1.0 / math.sqrt(2.0))))
    density = jnp.exp(-0.5 * value * value) * (1.0 / math.sqrt(2.0 * math.pi))
    return cdf_part + value * density

def reference(patches, pre_act, cotangent, w_up, w_down):
    values = patches.astype(jnp.float32)
    centre = lax.optimization_barrier(jnp.mean(values, axis=1, keepdims=True))
    spread = values - centre
    inv_std = lax.rsqrt(lax.optimization_barrier(jnp.mean(spread * spread, axis=1, keepdims=True)) + 1e-06)
    unit = spread * inv_std
    normed = unit.astype(jnp.bfloat16)
    grad_act = jnp.dot(cotangent, w_down.T, preferred_element_type=jnp.float32)
    factor = 1.0 / math.sqrt(TOKENS)
    grad_pre = (grad_act * gelu_slope(pre_act.astype(jnp.float32))).astype(jnp.bfloat16)
    grad_up = jnp.dot(normed.T, grad_pre, preferred_element_type=jnp.float32) * factor

    def add_group(group, total):
        offset = (group * FF_DEV).astype(jnp.int32)
        columns = lax.dynamic_slice_in_dim(w_up, offset, FF_DEV, 1)
        grads = lax.dynamic_slice_in_dim(grad_pre, offset, FF_DEV, 1)
        partial_sum = jnp.dot(grads, columns.T, preferred_element_type=jnp.float32)
        rounded = lax.optimization_barrier(partial_sum.astype(jnp.bfloat16))
        return total + rounded.astype(jnp.float32)
    grad_norm = lax.fori_loop(0, N_MP, add_group, jnp.zeros(values.shape, jnp.float32))
    first = lax.optimization_barrier(jnp.sum(grad_norm, axis=1, keepdims=True))
    second = lax.optimization_barrier(jnp.sum(grad_norm * unit, axis=1, keepdims=True))
    width = values.shape[1]
    result = cotangent.astype(jnp.float32) + inv_std * (grad_norm - first / width - unit * second / width)
    return (result.astype(jnp.bfloat16), grad_up)
```

```python
import math

import jax
import jax.numpy as jnp
from jax import lax
from jax.experimental import pallas as pl
from jax.experimental.pallas import tpu as pltpu
from jax.sharding import PartitionSpec as P

MESH = pl.DeviceIdType.MESH
F32 = jnp.float32
BF16 = jnp.bfloat16

NX, NY, NZ = 8, 8, 4


def gelu_slope(value):
    cdf_part = 0.5 * (1.0 + lax.erf(value * (1.0 / math.sqrt(2.0))))
    density = jnp.exp(-0.5 * value * value) * (1.0 / math.sqrt(2.0 * math.pi))
    return cdf_part + value * density


def add_bf16(a, b):
    return (a.astype(F32) + b.astype(F32)).astype(BF16)


class Counter:
    def __init__(self):
        self.n = 0

    def take(self):
        self.n += 1
        return self.n - 1


N_SEMS = 144


def kernel(
    patches, pre_act, cot, wu_hbm, wd_hbm, out_p, out_u,
    wu, wd, cbuf, nbuf, nts, slope, acc, gp, unit, q, qr, qz,
    x1, xr, zr1, z1, zr2, xr2, st1, st1r, st2, st2r,
    ssem, rsem, wsem,
):
    tok, fb = patches.shape
    d_all = fb * 2 * NY
    rb = fb // 4
    hid = pre_act.shape[1]
    cb = hid // 3
    scale = 1.0 / math.sqrt(tok * NX * NZ * 2)
    n_mp = 2 * NY
    ry, rx = NY // 2, NX // 2

    dp, mp = lax.axis_index("dp"), lax.axis_index("mp")
    c = lax.rem(dp, 2)
    x = lax.rem(dp // 2, NX)
    z = dp // (2 * NX)
    y, zh = mp // 2, lax.rem(mp, 2)

    def at_mp(off):
        return {"mp": lax.rem(mp + off, n_mp)}

    def at_y(off):
        return {"mp": lax.rem(y + off + NY, NY) * 2 + zh}

    def at_x(off):
        return {"dp": (z * NX + lax.rem(x + off + NX, NX)) * 2 + c}

    def at_z(off):
        return {"dp": (lax.rem(z + off, NZ) * NX + x) * 2 + c}

    partner = {"mp": y * 2 + 1 - zh}
    sibling = {"dp": dp + 1 - 2 * c}

    barrier = pltpu.get_barrier_semaphore()
    greeted = (
        [at_mp(k) for k in range(1, n_mp)]
        + [at_x(k) for k in range(1, NX)]
        + [at_z(k) for k in range(1, NZ)]
        + [sibling]
    )
    for peer in greeted:
        pl.semaphore_signal(barrier, inc=1, device_id=peer, device_id_type=MESH)

    load_wd = pltpu.make_async_copy(wd_hbm, wd, wsem.at[0])
    load_wu = pltpu.make_async_copy(wu_hbm, wu, wsem.at[1])
    load_wd.start()
    load_wu.start()

    counter = Counter()
    started = []

    def send(src, dst, peer):
        i = counter.take()
        copy = pltpu.make_async_remote_copy(
            src_ref=src, dst_ref=dst, send_sem=ssem.at[i], recv_sem=rsem.at[i],
            device_id=peer, device_id_type=MESH,
        )
        copy.start()
        started.append(copy)
        return copy

    cot_t = jnp.transpose(cot[...].astype(F32))
    cbuf[y, zh] = cot_t.astype(BF16).reshape(2, fb // 2, tok)
    pat_t = jnp.transpose(patches[...].astype(F32))
    total = jnp.sum(pat_t, axis=0, keepdims=True)
    off_centre = pat_t - total * (1.0 / fb)
    st1[...] = jnp.zeros_like(st1)
    st1[0:1, :] = total
    st1[1:2, :] = jnp.sum(off_centre * off_centre, axis=0, keepdims=True)
    unit[...] = pat_t
    acc[...] = jnp.zeros_like(acc)
    step = 128
    for i in range(hid // step):
        part = jnp.transpose(pre_act[:, i * step:(i + 1) * step].astype(F32))
        slope[i * step:(i + 1) * step, :] = gelu_slope(part)

    pl.semaphore_wait(barrier, len(greeted))

    def ag_start(buf, h, t):
        up, down = lax.rem(y - t + NY, NY), lax.rem(y + t, NY)
        if t < ry - 1:
            a, b = buf.at[up, h], buf.at[down, h]
        else:
            a, b = buf.at[up, h, 0], buf.at[down, h, 1]
        return send(a, a, at_y(1)), send(b, b, at_y(-1))

    stats = [send(st1, st1r.at[k - 1], at_mp(k)) for k in range(1, n_mp)]
    cot_swap = send(cbuf.at[y, zh], cbuf.at[y, zh], partner)
    cot_a = ag_start(cbuf, zh, 0)

    for copy in stats:
        copy.wait_recv()
    whole = st1[0:1, :]
    for k in range(n_mp - 1):
        whole = whole + st1r[k, 0:1, :]
    centre = whole * (1.0 / d_all)

    def block_square(sums, squares):
        shift = sums * (1.0 / fb) - centre
        return squares + fb * (shift * shift)

    square = block_square(st1[0:1, :], st1[1:2, :])
    for k in range(n_mp - 1):
        square = square + block_square(st1r[k, 0:1, :], st1r[k, 1:2, :])
    inv_std = lax.rsqrt(square * (1.0 / d_all) + 1e-06)
    unit[...] = (unit[...] - centre) * inv_std
    for par in range(2):
        for blk in range(2):
            lo = (2 * blk + par) * rb
            nts[par, blk * rb:(blk + 1) * rb, :] = unit[lo:lo + rb, :].astype(BF16)
    nbuf[y, zh, c] = nts[c]
    core_swap = send(nts.at[1 - c], nbuf.at[y, zh, c], sibling)

    cot_swap.wait_recv()
    cot_b = ag_start(cbuf, 1 - zh, 0)
    core_swap.wait_recv()
    n_swap = send(nbuf.at[y, zh], nbuf.at[y, zh], partner)
    n_a = ag_start(nbuf, zh, 0)
    load_wd.wait()

    def act_part(yp):
        lanes = pl.ds(pl.multiple_of(yp * (2 * fb), 128), 2 * fb)
        acc[...] += jnp.dot(
            wd[:, lanes], cbuf[yp].reshape(2 * fb, tok), preferred_element_type=F32
        )

    act_part(y)
    n_b = None
    for t in range(ry):
        last = t == ry - 1
        nxt = []
        for h, pair in ((zh, cot_a), (1 - zh, cot_b)):
            for copy in pair:
                copy.wait_recv()
            nxt.append(None if last else ag_start(cbuf, h, t + 1))
        cot_a, cot_b = nxt
        if not last:
            act_part(lax.rem(y - 1 - t + NY, NY))
            act_part(lax.rem(y + 1 + t, NY))
        else:
            act_part(lax.rem(y + ry, NY))
            own = (acc[...] * slope[...]).astype(BF16)
            gp[c] = own
            gp_swap = send(gp.at[c], gp.at[c], sibling)
        if t == 0:
            n_swap.wait_recv()
            n_b = ag_start(nbuf, 1 - zh, 0)
        nxt = []
        for h, pair in ((zh, n_a), (1 - zh, n_b)):
            for copy in pair:
                copy.wait_recv()
            nxt.append(None if last else ag_start(nbuf, h, t + 1))
        n_a, n_b = nxt

    load_wu.wait()
    for yp in range(NY):
        part = jnp.dot(
            wu[yp * 2 * fb:(yp + 1) * 2 * fb, :], own, preferred_element_type=F32
        )
        q[yp] = part.astype(BF16).reshape(2, fb, tok)
    far = lax.rem(y + ry, NY)
    y_up = send(q.at[far, 0], qr.at[0, 0, 0], at_y(1))
    y_down = send(q.at[far, 1], qr.at[1, 0, 1], at_y(-1))

    gp_swap.wait_recv()
    pair = jnp.concatenate([gp[0], gp[1]], axis=1)
    for yp in range(NY):
        rows = jnp.concatenate(
            [nbuf[yp, :, 0].reshape(fb, tok), nbuf[yp, :, 1].reshape(fb, tok)], axis=1
        )
        part = lax.dot_general(
            rows, pair, (((1,), (1,)), ((), ())), preferred_element_type=F32
        ).astype(BF16)
        for m in range(4):
            zp, xp = divmod(4 * yp + m, NX)
            block = part[m * rb:(m + 1) * rb, :]
            x1[0, xp, zp] = block[:, 0:cb]
            x1[1, xp, zp] = block[:, cb:2 * cb]
            z1[zp, xp] = block[:, 2 * cb:3 * cb]

    nh = NZ // 2
    xfar = lax.rem(x + rx, NX)
    x_up, x_down = [None] * 2, [None] * 2
    z_sends = []
    for s in range(2):
        x_up[s] = send(x1.at[s, xfar, pl.ds(0, nh)], xr.at[s, 0, 0, pl.ds(0, nh)], at_x(1))
        x_down[s] = send(x1.at[s, xfar, pl.ds(nh, nh)], xr.at[s, 1, 0, pl.ds(nh, nh)], at_x(-1))
    for k in range(1, NZ):
        z_sends.append(send(z1.at[lax.rem(z + k, NZ)], zr2.at[k - 1], at_z(k)))

    def y_round(t):
        up, down = lax.rem(y + ry - t, NY), lax.rem(y - ry + t + NY, NY)
        y_up.wait_recv()
        if t == 1:
            q[up, 0] = add_bf16(q[up, 0], qr[0, 0, 0])
        else:
            q[up] = add_bf16(q[up], qr[0, t - 1])
        a = send(q.at[up], qr.at[0, t], at_y(1))
        y_down.wait_recv()
        if t == 1:
            q[down, 1] = add_bf16(q[down, 1], qr[1, 0, 1])
        else:
            q[down] = add_bf16(q[down], qr[1, t - 1])
        return a, send(q.at[down], qr.at[1, t], at_y(-1))

    def x_round(s, t):
        up, down = lax.rem(x + rx - t, NX), lax.rem(x - rx + t + NX, NX)
        x_up[s].wait_recv()
        n = nh if t == 1 else NZ
        x1[s, up, 0:n] = add_bf16(x1[s, up, 0:n], xr[s, 0, t - 1, 0:n])
        x_up[s] = send(x1.at[s, up], xr.at[s, 0, t], at_x(1))
        x_down[s].wait_recv()
        n = nh if t == 1 else 0
        x1[s, down, n:NZ] = add_bf16(x1[s, down, n:NZ], xr[s, 1, t - 1, n:NZ])
        x_down[s] = send(x1.at[s, down], xr.at[s, 1, t], at_x(-1))

    for t in range(1, max(rx, ry)):
        if t < ry:
            y_up, y_down = y_round(t)
        if t < rx:
            for s in range(2):
                x_round(s, t)

    y_up.wait_recv()
    y_down.wait_recv()
    if ry == 1:
        q[y, 0] = add_bf16(q[y, 0], qr[0, 0, 0])
        q[y, 1] = add_bf16(q[y, 1], qr[1, 0, 1])
    else:
        q[y] = (
            q[y].astype(F32) + qr[0, ry - 1].astype(F32) + qr[1, ry - 1].astype(F32)
        ).astype(BF16)
    q_swap = send(q.at[y, 1 - zh], qz, partner)

    out1 = []
    for s in range(2):
        x_up[s].wait_recv()
        x_down[s].wait_recv()
        x1[s, x] = (
            x1[s, x].astype(F32) + xr[s, 0, rx - 1].astype(F32) + xr[s, 1, rx - 1].astype(F32)
        ).astype(BF16)
        out1.append(
            [send(x1.at[s, x, lax.rem(z + k, NZ)], zr1.at[s, k - 1], at_z(k)) for k in range(1, NZ)]
        )

    q_swap.wait_recv()
    grad_norm = q[y, zh].astype(F32) + qz[...].astype(F32)
    st2[...] = jnp.zeros_like(st2)
    st2[0:1, :] = jnp.sum(grad_norm, axis=0, keepdims=True)
    st2[1:2, :] = jnp.sum(grad_norm * unit[...], axis=0, keepdims=True)
    stats = [send(st2, st2r.at[k - 1], at_mp(k)) for k in range(1, n_mp)]

    for copy in z_sends:
        copy.wait_recv()
    z_sum = z1[z].astype(F32)
    for k in range(NZ - 1):
        z_sum = z_sum + zr2[k].astype(F32)
    z1[z] = z_sum.astype(BF16)
    out2 = [send(z1.at[z, lax.rem(x + k, NX)], xr2.at[k - 1], at_x(k)) for k in range(1, NX)]

    for copy in stats:
        copy.wait_recv()
    both = st2[...]
    for k in range(n_mp - 1):
        both = both + st2r[k]
    first, second = both[0:1, :] * (1.0 / d_all), both[1:2, :] * (1.0 / d_all)
    result = cbuf[y, zh].reshape(fb, tok).astype(F32) + inv_std * (
        grad_norm - first - unit[...] * second
    )
    out_p[...] = jnp.transpose(result).astype(BF16)

    for s in range(2):
        block = x1[s, x, z].astype(F32)
        for k, copy in enumerate(out1[s]):
            copy.wait_recv()
            block = block + zr1[s, k].astype(F32)
        out_u[:, s * cb:(s + 1) * cb] = block * scale
    block = z1[z, x].astype(F32)
    for k, copy in enumerate(out2):
        copy.wait_recv()
        block = block + xr2[k].astype(F32)
    out_u[:, 2 * cb:3 * cb] = block * scale

    for copy in started:
        copy.wait_send()


def per_device(patches, pre_act, cotangent, w_up, w_down):
    tok, fb = patches.shape
    hid = pre_act.shape[1]
    d_all = w_up.shape[0]
    rb, cb = fb // 4, hid // 3
    ry, rx = NY // 2, NX // 2
    vmem = pl.BlockSpec(memory_space=pltpu.VMEM)
    anywhere = pl.BlockSpec(memory_space=pl.ANY)
    return pl.pallas_call(
        kernel,
        out_shape=(
            jax.ShapeDtypeStruct((tok, fb), BF16),
            jax.ShapeDtypeStruct((rb, hid), F32),
        ),
        in_specs=[vmem, vmem, vmem, anywhere, anywhere],
        out_specs=(vmem, vmem),
        scratch_shapes=[
            pltpu.VMEM((d_all, hid), BF16),
            pltpu.VMEM((hid, d_all), BF16),
            pltpu.VMEM((NY, 2, 2, fb // 2, tok), BF16),
            pltpu.VMEM((NY, 2, 2, fb // 2, tok), BF16),
            pltpu.VMEM((2, fb // 2, tok), BF16),
            pltpu.VMEM((hid, tok), F32),
            pltpu.VMEM((hid, tok), F32),
            pltpu.VMEM((2, hid, tok), BF16),
            pltpu.VMEM((fb, tok), F32),
            pltpu.VMEM((NY, 2, fb, tok), BF16),
            pltpu.VMEM((2, ry, 2, fb, tok), BF16),
            pltpu.VMEM((fb, tok), BF16),
            pltpu.VMEM((2, NX, NZ, rb, cb), BF16),
            pltpu.VMEM((2, 2, rx, NZ, rb, cb), BF16),
            pltpu.VMEM((2, NZ - 1, rb, cb), BF16),
            pltpu.VMEM((NZ, NX, rb, cb), BF16),
            pltpu.VMEM((NZ - 1, NX, rb, cb), BF16),
            pltpu.VMEM((NX - 1, rb, cb), BF16),
            pltpu.VMEM((8, tok), F32),
            pltpu.VMEM((2 * NY - 1, 8, tok), F32),
            pltpu.VMEM((8, tok), F32),
            pltpu.VMEM((2 * NY - 1, 8, tok), F32),
            pltpu.SemaphoreType.DMA((N_SEMS,)),
            pltpu.SemaphoreType.DMA((N_SEMS,)),
            pltpu.SemaphoreType.DMA((2,)),
        ],
        compiler_params=pltpu.CompilerParams(
            collective_id=0, has_side_effects=True, vmem_limit_bytes=48 * 1024 * 1024
        ),
        cost_estimate=pl.CostEstimate(
            flops=6 * tok * d_all * hid, bytes_accessed=4 * d_all * hid, transcendentals=2 * tok * hid
        ),
    )(patches, pre_act, cotangent, w_up, w_down)


def solution(mesh):
    return jax.shard_map(
        per_device,
        mesh=mesh,
        in_specs=(P("dp", "mp"), P("dp", "mp"), P("dp", "mp"), P(None, "mp"), P("mp", None)),
        out_specs=(P("dp", "mp"), P("dp", "mp")),
        check_vma=False,
    )
```

```python
import math

import jax
import jax.numpy as jnp
from jax import lax
from jax.experimental import pallas as pl
from jax.experimental.pallas import tpu as pltpu
from jax.sharding import PartitionSpec as P

MESH = pl.DeviceIdType.MESH
F32 = jnp.float32
BF16 = jnp.bfloat16

NX, NY, NZ = 8, 8, 4


def gelu_slope(value):
    cdf_part = 0.5 * (1.0 + lax.erf(value * (1.0 / math.sqrt(2.0))))
    density = jnp.exp(-0.5 * value * value) * (1.0 / math.sqrt(2.0 * math.pi))
    return cdf_part + value * density


def add_bf16(a, b):
    return (a.astype(F32) + b.astype(F32)).astype(BF16)


class Counter:
    def __init__(self):
        self.n = 0

    def take(self):
        self.n += 1
        return self.n - 1


N_SEMS = 144


def kernel(
    patches, pre_hbm, cot, wu_hbm, wd_hbm, out_p, out_u,
    wu, wd, pre_act, cbuf, nbuf, nts, slope, acc, gp, unit, q, qr, qz,
    x1, xr, zr1, z1, zr2, xr2, st1, st1r, st2, st2r,
    ssem, rsem, wsem,
):
    fb, tok = patches.shape
    d_all = fb * 2 * NY
    rb = fb // 4
    hid = pre_act.shape[1]
    cb = hid // 3
    scale = 1.0 / math.sqrt(tok * NX * NZ * 2)
    n_mp = 2 * NY
    ry, rx = NY // 2, NX // 2

    dp, mp = lax.axis_index("dp"), lax.axis_index("mp")
    c = lax.rem(dp, 2)
    x = lax.rem(dp // 2, NX)
    z = dp // (2 * NX)
    y, zh = mp // 2, lax.rem(mp, 2)

    def at_mp(off):
        return {"mp": lax.rem(mp + off, n_mp)}

    def at_y(off):
        return {"mp": lax.rem(y + off + NY, NY) * 2 + zh}

    def at_x(off):
        return {"dp": (z * NX + lax.rem(x + off + NX, NX)) * 2 + c}

    def at_z(off):
        return {"dp": (lax.rem(z + off, NZ) * NX + x) * 2 + c}

    partner = {"mp": y * 2 + 1 - zh}
    sibling = {"dp": dp + 1 - 2 * c}

    barrier = pltpu.get_barrier_semaphore()
    greeted = (
        [at_mp(k) for k in range(1, n_mp)]
        + [at_x(k) for k in range(1, NX)]
        + [at_z(k) for k in range(1, NZ)]
        + [sibling]
    )
    for peer in greeted:
        pl.semaphore_signal(barrier, inc=1, device_id=peer, device_id_type=MESH)

    load_wd = pltpu.make_async_copy(wd_hbm, wd, wsem.at[0])
    load_wu = pltpu.make_async_copy(wu_hbm, wu, wsem.at[1])
    load_pre = pltpu.make_async_copy(pre_hbm, pre_act, wsem.at[2])
    load_pre.start()
    load_wd.start()
    load_wu.start()

    counter = Counter()
    started = []

    def send(src, dst, peer):
        i = counter.take()
        copy = pltpu.make_async_remote_copy(
            src_ref=src, dst_ref=dst, send_sem=ssem.at[i], recv_sem=rsem.at[i],
            device_id=peer, device_id_type=MESH,
        )
        copy.start()
        started.append(copy)
        return copy

    def ag_start(buf, h, t, own=None):
        up, down = lax.rem(y - t + NY, NY), lax.rem(y + t, NY)
        if t < ry - 1:
            a, b = buf.at[up, h], buf.at[down, h]
        else:
            a, b = buf.at[up, h, 0], buf.at[down, h, 1]
        if own is None:
            return send(a, a, at_y(1)), send(b, b, at_y(-1))
        if t < ry - 1:
            return send(own, a, at_y(1)), send(own, b, at_y(-1))
        return send(own.at[0], a, at_y(1)), send(own.at[1], b, at_y(-1))

    pat = patches[...].astype(F32)
    total = jnp.sum(pat, axis=0, keepdims=True)
    off_centre = pat - total * (1.0 / fb)
    st1[...] = jnp.zeros_like(st1)
    st1[0:1, :] = total
    st1[1:2, :] = jnp.sum(off_centre * off_centre, axis=0, keepdims=True)

    pl.semaphore_wait(barrier, len(greeted))

    cot_swap = send(cot, cbuf.at[y, zh], partner)
    cot_a = ag_start(cbuf, zh, 0, cot)
    stats = [send(st1, st1r.at[k - 1], at_mp(k)) for k in range(1, n_mp)]

    cbuf[y, zh] = cot[...]
    step = 128

    def slopes(lo, hi):
        for i in range(lo, hi):
            part = jnp.transpose(pre_act[:, i * step:(i + 1) * step].astype(F32))
            slope[i * step:(i + 1) * step, :] = gelu_slope(part)

    def act_part(yp, first=False):
        lanes = pl.ds(pl.multiple_of(yp * (2 * fb), 128), 2 * fb)
        part = jnp.dot(wd[:, lanes], cbuf[yp].reshape(2 * fb, tok), preferred_element_type=F32)
        acc[...] = part if first else acc[...] + part

    def act_round(t):
        if t < ry - 1:
            act_part(lax.rem(y - 1 - t + NY, NY))
            act_part(lax.rem(y + 1 + t, NY))
        else:
            act_part(lax.rem(y + ry, NY))

    def pass_on(buf, h, copies, t):
        for copy in copies:
            copy.wait_recv()
        return None if t == ry - 1 else ag_start(buf, h, t + 1)

    load_pre.wait()
    slopes(0, hid // step // 2)
    cot_a = pass_on(cbuf, zh, cot_a, 0)
    cot_swap.wait_recv()
    cot_b = ag_start(cbuf, 1 - zh, 0)
    load_wd.wait()
    act_part(y, True)
    slopes(hid // step // 2, hid // step)

    for copy in stats:
        copy.wait_recv()
    whole = st1[0:1, :]
    for k in range(n_mp - 1):
        whole = whole + st1r[k, 0:1, :]
    centre = whole * (1.0 / d_all)

    def block_square(sums, squares):
        shift = sums * (1.0 / fb) - centre
        return squares + fb * (shift * shift)

    square = block_square(st1[0:1, :], st1[1:2, :])
    for k in range(n_mp - 1):
        square = square + block_square(st1r[k, 0:1, :], st1r[k, 1:2, :])
    inv_std = lax.rsqrt(square * (1.0 / d_all) + 1e-06)
    unit[...] = (patches[...].astype(F32) - centre) * inv_std
    for par in range(2):
        for blk in range(2):
            lo = (2 * blk + par) * rb
            nts[par, blk * rb:(blk + 1) * rb, :] = unit[lo:lo + rb, :].astype(BF16)
    core_swap = send(nts.at[1 - c], nbuf.at[y, zh, c], sibling)
    nbuf[y, zh, c] = nts[c]

    n_a = n_b = n_swap = None
    n_step = 0
    for t in range(ry):
        if t > 0:
            cot_a = pass_on(cbuf, zh, cot_a, t)
        cot_b = pass_on(cbuf, 1 - zh, cot_b, t)
        if t == min(1, ry - 1):
            core_swap.wait_recv()
            n_swap = send(nbuf.at[y, zh], nbuf.at[y, zh], partner)
            n_a = ag_start(nbuf, zh, 0)
        if t == 2:
            n_a = pass_on(nbuf, zh, n_a, 0)
            n_swap.wait_recv()
            n_b = ag_start(nbuf, 1 - zh, 0)
            n_step = 1
        act_round(t)
    own = acc[...] * slope[...]
    gp[c] = jnp.transpose(own).astype(BF16)
    gp_swap = send(gp.at[c], gp.at[c], sibling)
    own = own.astype(BF16)
    if n_b is None:
        n_swap.wait_recv()
        n_b = ag_start(nbuf, 1 - zh, 0)

    def up_part(yp):
        rows = jnp.concatenate(
            [nbuf[yp, :, 0].reshape(fb, tok), nbuf[yp, :, 1].reshape(fb, tok)], axis=1
        )
        part = jnp.dot(
            rows, gp[...].reshape(2 * tok, hid), preferred_element_type=F32
        ).astype(BF16)
        for m in range(4):
            zp, xp = (4 * yp + m) // NX, lax.rem(4 * yp + m, NX)
            block = part[m * rb:(m + 1) * rb, :]
            x1[0, xp, zp] = block[:, 0:cb]
            x1[1, xp, zp] = block[:, cb:2 * cb]
            z1[zp, xp] = block[:, 2 * cb:3 * cb]

    for t in range(ry):
        if t >= n_step:
            n_a = pass_on(nbuf, zh, n_a, t)
        n_b = pass_on(nbuf, 1 - zh, n_b, t)
        if t == 0:
            gp_swap.wait_recv()
            up_part(y)
        if t < ry - 1:
            up_part(lax.rem(y - 1 - t + NY, NY))
            up_part(lax.rem(y + 1 + t, NY))
        else:
            up_part(lax.rem(y + ry, NY))

    nh = NZ // 2
    xfar = lax.rem(x + rx, NX)
    x_up, x_down = [None] * 2, [None] * 2
    z_sends = []
    for s in range(2):
        x_up[s] = send(x1.at[s, xfar, pl.ds(0, nh)], xr.at[s, 0, 0, pl.ds(0, nh)], at_x(1))
        x_down[s] = send(x1.at[s, xfar, pl.ds(nh, nh)], xr.at[s, 1, 0, pl.ds(nh, nh)], at_x(-1))
        if s == 0:
            for k in range(1, NZ):
                z_sends.append(send(z1.at[lax.rem(z + k, NZ)], zr2.at[k - 1], at_z(k)))

    load_wu.wait()
    for yp in range(NY):
        part = jnp.dot(
            wu[yp * 2 * fb:(yp + 1) * 2 * fb, :], own, preferred_element_type=F32
        )
        q[yp] = part.astype(BF16).reshape(2, fb, tok)
    far = lax.rem(y + ry, NY)
    y_up = send(q.at[far, 0], qr.at[0, 0, 0], at_y(1))
    y_down = send(q.at[far, 1], qr.at[1, 0, 1], at_y(-1))

    def y_round(t):
        up, down = lax.rem(y + ry - t, NY), lax.rem(y - ry + t + NY, NY)
        y_up.wait_recv()
        if t == 1:
            q[up, 0] = add_bf16(q[up, 0], qr[0, 0, 0])
        else:
            q[up] = add_bf16(q[up], qr[0, t - 1])
        a = send(q.at[up], qr.at[0, t], at_y(1))
        y_down.wait_recv()
        if t == 1:
            q[down, 1] = add_bf16(q[down, 1], qr[1, 0, 1])
        else:
            q[down] = add_bf16(q[down], qr[1, t - 1])
        return a, send(q.at[down], qr.at[1, t], at_y(-1))

    def x_round(s, t):
        up, down = lax.rem(x + rx - t, NX), lax.rem(x - rx + t + NX, NX)
        x_up[s].wait_recv()
        n = nh if t == 1 else NZ
        x1[s, up, 0:n] = add_bf16(x1[s, up, 0:n], xr[s, 0, t - 1, 0:n])
        x_up[s] = send(x1.at[s, up], xr.at[s, 0, t], at_x(1))
        x_down[s].wait_recv()
        n = nh if t == 1 else 0
        x1[s, down, n:NZ] = add_bf16(x1[s, down, n:NZ], xr[s, 1, t - 1, n:NZ])
        x_down[s] = send(x1.at[s, down], xr.at[s, 1, t], at_x(-1))

    def y_last():
        y_up.wait_recv()
        y_down.wait_recv()
        if ry == 1:
            q[y, 0] = add_bf16(q[y, 0], qr[0, 0, 0])
            q[y, 1] = add_bf16(q[y, 1], qr[1, 0, 1])
        else:
            q[y] = (
                q[y].astype(F32) + qr[0, ry - 1].astype(F32) + qr[1, ry - 1].astype(F32)
            ).astype(BF16)
        return send(q.at[y, 1 - zh], qz, partner)

    x_steps = [(s, t) for t in range(1, rx) for s in range(2)]
    y_steps = list(range(1, ry)) + ["last"]
    y_after = [1, 2, 3, 4]
    done = 0
    for i, (s, t) in enumerate(x_steps):
        x_round(s, t)
        if done < len(y_steps) and i >= y_after[done]:
            if y_steps[done] == "last":
                q_swap = y_last()
            else:
                y_up, y_down = y_round(y_steps[done])
            done += 1
    for step in y_steps[done:]:
        if step == "last":
            q_swap = y_last()
        else:
            y_up, y_down = y_round(step)

    out1 = []
    for s in range(2):
        x_up[s].wait_recv()
        x_down[s].wait_recv()
        x1[s, x] = (
            x1[s, x].astype(F32) + xr[s, 0, rx - 1].astype(F32) + xr[s, 1, rx - 1].astype(F32)
        ).astype(BF16)
        out1.append(
            [send(x1.at[s, x, lax.rem(z + k, NZ)], zr1.at[s, k - 1], at_z(k)) for k in range(1, NZ)]
        )

    for copy in z_sends:
        copy.wait_recv()
    z_sum = z1[z].astype(F32)
    for k in range(NZ - 1):
        z_sum = z_sum + zr2[k].astype(F32)
    z1[z] = z_sum.astype(BF16)
    out2 = [send(z1.at[z, lax.rem(x + k, NX)], xr2.at[k - 1], at_x(k)) for k in range(1, NX)]

    q_swap.wait_recv()
    grad_norm = q[y, zh].astype(F32) + qz[...].astype(F32)
    st2[...] = jnp.zeros_like(st2)
    st2[0:1, :] = jnp.sum(grad_norm, axis=0, keepdims=True)
    st2[1:2, :] = jnp.sum(grad_norm * unit[...], axis=0, keepdims=True)
    stats = [send(st2, st2r.at[k - 1], at_mp(k)) for k in range(1, n_mp)]

    for s in range(2):
        block = x1[s, x, z].astype(F32)
        for k, copy in enumerate(out1[s]):
            copy.wait_recv()
            block = block + zr1[s, k].astype(F32)
        out_u[:, s * cb:(s + 1) * cb] = block * scale

    for copy in stats:
        copy.wait_recv()
    both = st2[...]
    for k in range(n_mp - 1):
        both = both + st2r[k]
    first, second = both[0:1, :] * (1.0 / d_all), both[1:2, :] * (1.0 / d_all)
    result = cot[...].reshape(fb, tok).astype(F32) + inv_std * (
        grad_norm - first - unit[...] * second
    )
    out_p[...] = result.astype(BF16)

    block = z1[z, x].astype(F32)
    for k, copy in enumerate(out2):
        copy.wait_recv()
        block = block + xr2[k].astype(F32)
    out_u[:, 2 * cb:3 * cb] = block * scale

    for copy in started:
        copy.wait_send()


def per_device(patches, pre_act, cotangent, w_up, w_down):
    tok, fb = patches.shape
    hid = pre_act.shape[1]
    d_all = w_up.shape[0]
    rb, cb = fb // 4, hid // 3
    rx, ry = NX // 2, NY // 2
    vmem = pl.BlockSpec(memory_space=pltpu.VMEM)
    anywhere = pl.BlockSpec(memory_space=pltpu.HBM)
    grad_t, grad_up = pl.pallas_call(
        kernel,
        out_shape=(
            jax.ShapeDtypeStruct((fb, tok), BF16),
            jax.ShapeDtypeStruct((rb, hid), F32),
        ),
        in_specs=[vmem, anywhere, vmem, anywhere, anywhere],
        out_specs=(vmem, vmem),
        scratch_shapes=[
            pltpu.VMEM((d_all, hid), BF16),
            pltpu.VMEM((hid, d_all), BF16),
            pltpu.VMEM((tok, hid), BF16),
            pltpu.VMEM((NY, 2, 2, fb // 2, tok), BF16),
            pltpu.VMEM((NY, 2, 2, fb // 2, tok), BF16),
            pltpu.VMEM((2, fb // 2, tok), BF16),
            pltpu.VMEM((hid, tok), F32),
            pltpu.VMEM((hid, tok), F32),
            pltpu.VMEM((2, tok, hid), BF16),
            pltpu.VMEM((fb, tok), F32),
            pltpu.VMEM((NY, 2, fb, tok), BF16),
            pltpu.VMEM((2, ry, 2, fb, tok), BF16),
            pltpu.VMEM((fb, tok), BF16),
            pltpu.VMEM((2, NX, NZ, rb, cb), BF16),
            pltpu.VMEM((2, 2, rx, NZ, rb, cb), BF16),
            pltpu.VMEM((2, NZ - 1, rb, cb), BF16),
            pltpu.VMEM((NZ, NX, rb, cb), BF16),
            pltpu.VMEM((NZ - 1, NX, rb, cb), BF16),
            pltpu.VMEM((NX - 1, rb, cb), BF16),
            pltpu.VMEM((8, tok), F32),
            pltpu.VMEM((2 * NY - 1, 8, tok), F32),
            pltpu.VMEM((8, tok), F32),
            pltpu.VMEM((2 * NY - 1, 8, tok), F32),
            pltpu.SemaphoreType.DMA((N_SEMS,)),
            pltpu.SemaphoreType.DMA((N_SEMS,)),
            pltpu.SemaphoreType.DMA((3,)),
        ],
        compiler_params=pltpu.CompilerParams(
            collective_id=0, has_side_effects=True, vmem_limit_bytes=62 * 1024 * 1024
        ),
        cost_estimate=pl.CostEstimate(
            flops=6 * tok * d_all * hid, bytes_accessed=4 * d_all * hid, transcendentals=2 * tok * hid
        ),
    )(patches.T, pre_act, cotangent.T.reshape(2, fb // 2, tok), w_up, w_down)
    return grad_t.T, grad_up


def solution(mesh):
    return jax.shard_map(
        per_device,
        mesh=mesh,
        in_specs=(P("dp", "mp"), P("dp", "mp"), P("dp", "mp"), P(None, "mp"), P("mp", None)),
        out_specs=(P("dp", "mp"), P("dp", "mp")),
        check_vma=False,
    )
```

```python
import math

import jax
import jax.numpy as jnp
from jax import lax
from jax.experimental import pallas as pl
from jax.experimental.pallas import tpu as pltpu
from jax.sharding import PartitionSpec as P

MESH = pl.DeviceIdType.MESH
F32 = jnp.float32
BF16 = jnp.bfloat16

NX, NY, NZ = 8, 8, 4


def gelu_slope(value):
    cdf_part = 0.5 * (1.0 + lax.erf(value * (1.0 / math.sqrt(2.0))))
    density = jnp.exp(-0.5 * value * value) * (1.0 / math.sqrt(2.0 * math.pi))
    return cdf_part + value * density


def add_bf16(a, b):
    return (a.astype(F32) + b.astype(F32)).astype(BF16)


class Counter:
    def __init__(self):
        self.n = 0

    def take(self):
        self.n += 1
        return self.n - 1


N_SEMS = 144


def kernel(
    patches, pre_hbm, cot, wu_hbm, wd_hbm, out_p, out_u,
    wu, wd, pre_act, cbuf, nbuf, pats, pbuf, slope, acc, gp, unit, q, qr, qz, qsum,
    x1, xr, zr1, z1, zr2, xr2, lnp, st1, st1r, st2, st2r, st3, st3r,
    ssem, rsem, wsem,
):
    fb, tok = patches.shape
    d_all = fb * 2 * NY
    rb = fb // 4
    hid = pre_act.shape[1]
    cb = hid // 3
    scale = 1.0 / math.sqrt(tok * NX * NZ * 2)
    ry, rx = NY // 2, NX // 2

    dp, mp = lax.axis_index("dp"), lax.axis_index("mp")
    c = lax.rem(dp, 2)
    x = lax.rem(dp // 2, NX)
    z = dp // (2 * NX)
    y, zh = mp // 2, lax.rem(mp, 2)

    def at_y(off):
        return {"mp": lax.rem(y + off + NY, NY) * 2 + zh}

    def at_x(off):
        return {"dp": (z * NX + lax.rem(x + off + NX, NX)) * 2 + c}

    def at_z(off):
        return {"dp": (lax.rem(z + off, NZ) * NX + x) * 2 + c}

    partner = {"mp": y * 2 + 1 - zh}
    sibling = {"dp": dp + 1 - 2 * c}

    barrier = pltpu.get_barrier_semaphore()
    greeted = (
        [at_y(k) for k in range(1, NY)]
        + [at_x(k) for k in range(1, NX)]
        + [at_z(k) for k in range(1, NZ)]
        + [sibling, partner]
    )
    for peer in greeted:
        pl.semaphore_signal(barrier, inc=1, device_id=peer, device_id_type=MESH)

    def loads(src, dst, first):
        n = src.shape[0] // 4
        return [
            pltpu.make_async_copy(
                src.at[pl.ds(i * n, n)], dst.at[pl.ds(i * n, n)], wsem.at[first + i]
            )
            for i in range(4)
        ]

    load_pre = pltpu.make_async_copy(pre_hbm, pre_act, wsem.at[8])
    load_wd, load_wu = loads(wd_hbm, wd, 0), loads(wu_hbm, wu, 4)
    for copy in [load_pre] + load_wd:
        copy.start()

    counter = Counter()
    started = []

    def send(src, dst, peer):
        i = counter.take()
        copy = pltpu.make_async_remote_copy(
            src_ref=src, dst_ref=dst, send_sem=ssem.at[i], recv_sem=rsem.at[i],
            device_id=peer, device_id_type=MESH,
        )
        copy.start()
        started.append(copy)
        return copy

    def ag_start(buf, h, t, own=None):
        up, down = lax.rem(y - t + NY, NY), lax.rem(y + t, NY)
        if t < ry - 1:
            a, b = buf.at[up, h], buf.at[down, h]
        else:
            a, b = buf.at[up, h, 0], buf.at[down, h, 1]
        if own is None:
            return send(a, a, at_y(1)), send(b, b, at_y(-1))
        if t < ry - 1:
            return send(own, a, at_y(1)), send(own, b, at_y(-1))
        return send(own.at[0], a, at_y(1)), send(own.at[1], b, at_y(-1))

    for par in range(2):
        for blk in range(2):
            lo = (2 * blk + par) * rb
            pats[par, blk * rb:(blk + 1) * rb, :] = patches[lo:lo + rb, :]

    pl.semaphore_wait(barrier, len(greeted))

    cot_swap = send(cot, cbuf.at[y, zh], partner)
    core_swap = send(pats.at[1 - c], nbuf.at[y, zh, c], sibling)
    cot_a = ag_start(cbuf, zh, 0, cot)
    pat_swap = [send(pats.at[c], nbuf.at[y, zh, c], partner)]
    nbuf[y, zh, c] = pats[c]

    cbuf[y, zh] = cot[...]
    step = 128

    def slopes(lo, hi):
        for i in range(lo, hi):
            part = jnp.transpose(pre_act[:, i * step:(i + 1) * step].astype(F32))
            slope[i * step:(i + 1) * step, :] = gelu_slope(part)

    def act_part(yp, first=False):
        lanes = pl.ds(pl.multiple_of(yp * (2 * fb), 128), 2 * fb)
        part = jnp.dot(wd[:, lanes], cbuf[yp].reshape(2 * fb, tok), preferred_element_type=F32)
        acc[...] = part if first else acc[...] + part

    def act_round(t):
        if t < ry - 1:
            act_part(lax.rem(y - 1 - t + NY, NY))
            act_part(lax.rem(y + 1 + t, NY))
        else:
            act_part(lax.rem(y + ry, NY))

    def pass_on(buf, h, copies, t):
        for copy in copies:
            copy.wait_recv()
        return None if t == ry - 1 else ag_start(buf, h, t + 1)

    def norm_part(yp):
        for k in range(2):
            block = nbuf[yp, :, k].reshape(fb, tok).astype(F32)
            total = jnp.sum(block, axis=0, keepdims=True)
            off = block - total * (1.0 / fb)
            lnp[yp, k:k + 1, :] = total
            lnp[yp, 2 + k:3 + k, :] = jnp.sum(off * off, axis=0, keepdims=True)

    def norm_round(t):
        if t < ry - 1:
            norm_part(lax.rem(y - 1 - t + NY, NY))
            norm_part(lax.rem(y + 1 + t, NY))
        else:
            norm_part(lax.rem(y + ry, NY))

    core_swap.wait_recv()
    pat_swap.append(send(nbuf.at[y, zh, 1 - c], nbuf.at[y, zh, 1 - c], partner))
    pat_a = ag_start(nbuf, zh, 0)
    load_pre.wait()
    slopes(0, hid // step)
    for t in range(ry + 1):
        if t < ry:
            cot_a = pass_on(cbuf, zh, cot_a, t)
            pat_a = pass_on(nbuf, zh, pat_a, t)
        if t == 0:
            cot_swap.wait_recv()
            cot_b = ag_start(cbuf, 1 - zh, 0)
            for copy in pat_swap:
                copy.wait_recv()
            pat_b = ag_start(nbuf, 1 - zh, 0)
            other_rows = send(nbuf.at[y, 1 - zh, 1 - c], pbuf, sibling)
            norm_part(y)
        else:
            cot_b = pass_on(cbuf, 1 - zh, cot_b, t - 1)
            if t < ry:
                pat_b = pass_on(nbuf, 1 - zh, pat_b, t - 1)
            if t == 1:
                for copy in load_wd:
                    copy.wait()
                for copy in load_wu:
                    copy.start()
                act_part(y, True)
            if t < ry:
                act_round(t - 1)
                norm_round(t - 1)
    act_round(ry - 1)
    own = acc[...] * slope[...]
    gp[c] = jnp.transpose(own).astype(BF16)
    gp_swap = send(gp.at[c], gp.at[c], sibling)
    own = own.astype(BF16)
    pass_on(nbuf, 1 - zh, pat_b, ry - 1)
    norm_round(ry - 1)

    def combine(parts, count):
        whole = parts[0][0]
        for sums, _ in parts[1:]:
            whole = whole + sums
        mean = whole * (1.0 / (count * len(parts)))
        square = None
        for sums, squares in parts:
            shift = sums * (1.0 / count) - mean
            term = squares + count * (shift * shift)
            square = term if square is None else square + term
        return whole, square

    here = combine([(lnp[yp, 0:2, :], lnp[yp, 2:4, :]) for yp in range(NY)], fb)
    st1[...] = jnp.zeros_like(st1)
    st1[0:2, :], st1[2:4, :] = here
    norm_swap = send(st1, st1r, sibling)

    for copy in load_wu:
        copy.wait()
    for yp in range(NY):
        part = jnp.dot(
            wu[yp * 2 * fb:(yp + 1) * 2 * fb, :], own, preferred_element_type=F32
        )
        q[yp] = part.astype(BF16).reshape(2, fb, tok)
    far = lax.rem(y + ry, NY)
    y_up = send(q.at[far, 0], qr.at[0, 0, 0], at_y(1))
    y_down = send(q.at[far, 1], qr.at[1, 0, 1], at_y(-1))

    norm_swap.wait_recv()
    whole, square = combine([here, (st1r[0:2, :], st1r[2:4, :])], d_all // 2)
    centres = whole * (1.0 / d_all)
    inv_stds = lax.rsqrt(square * (1.0 / d_all) + 1e-06)
    centre = jnp.where(c == 0, centres[0:1, :], centres[1:2, :])
    inv_std = jnp.where(c == 0, inv_stds[0:1, :], inv_stds[1:2, :])

    def up_part(yp):
        rows = [
            (nbuf[yp, :, k].reshape(fb, tok).astype(F32) - centres[k:k + 1, :])
            * inv_stds[k:k + 1, :]
            for k in range(2)
        ]
        part = jnp.dot(
            jnp.concatenate(rows, axis=1).astype(BF16),
            gp[...].reshape(2 * tok, hid),
            preferred_element_type=F32,
        ).astype(BF16)
        for m in range(4):
            zp, xp = divmod(4 * yp + m, NX)
            block = part[m * rb:(m + 1) * rb, :]
            x1[0, xp, zp] = block[:, 0:cb]
            x1[1, xp, zp] = block[:, cb:2 * cb]
            z1[zp, xp] = block[:, 2 * cb:3 * cb]

    gp_swap.wait_recv()
    for yp in range(NY):
        up_part(yp)

    nh = NZ // 2
    xfar = lax.rem(x + rx, NX)
    x_up, x_down = [None] * 2, [None] * 2
    z_sends = []
    for s in range(2):
        x_up[s] = send(x1.at[s, xfar, pl.ds(0, nh)], xr.at[s, 0, 0, pl.ds(0, nh)], at_x(1))
        x_down[s] = send(x1.at[s, xfar, pl.ds(nh, nh)], xr.at[s, 1, 0, pl.ds(nh, nh)], at_x(-1))
        if s == 0:
            for k in range(1, NZ):
                z_sends.append(send(z1.at[lax.rem(z + k, NZ)], zr2.at[k - 1], at_z(k)))

    def y_round(t):
        up, down = lax.rem(y + ry - t, NY), lax.rem(y - ry + t + NY, NY)
        y_up.wait_recv()
        if t == 1:
            q[up, 0] = add_bf16(q[up, 0], qr[0, 0, 0])
        else:
            q[up] = add_bf16(q[up], qr[0, t - 1])
        a = send(q.at[up], qr.at[0, t], at_y(1))
        y_down.wait_recv()
        if t == 1:
            q[down, 1] = add_bf16(q[down, 1], qr[1, 0, 1])
        else:
            q[down] = add_bf16(q[down], qr[1, t - 1])
        return a, send(q.at[down], qr.at[1, t], at_y(-1))

    def x_round(s, t):
        up, down = lax.rem(x + rx - t, NX), lax.rem(x - rx + t + NX, NX)
        x_up[s].wait_recv()
        n = nh if t == 1 else NZ
        x1[s, up, 0:n] = add_bf16(x1[s, up, 0:n], xr[s, 0, t - 1, 0:n])
        x_up[s] = send(x1.at[s, up], xr.at[s, 0, t], at_x(1))
        x_down[s].wait_recv()
        n = nh if t == 1 else 0
        x1[s, down, n:NZ] = add_bf16(x1[s, down, n:NZ], xr[s, 1, t - 1, n:NZ])
        x_down[s] = send(x1.at[s, down], xr.at[s, 1, t], at_x(-1))

    def unit_of(block):
        return (block.astype(F32) - centre) * inv_std

    def y_last():
        y_up.wait_recv()
        y_down.wait_recv()
        if ry == 1:
            qsum[0] = q[y, 0].astype(F32) + qr[0, 0, 0].astype(F32)
            qsum[1] = q[y, 1].astype(F32) + qr[1, 0, 1].astype(F32)
        else:
            qsum[...] = (
                q[y].astype(F32) + qr[0, ry - 1].astype(F32) + qr[1, ry - 1].astype(F32)
            )
        q[y, 1 - zh] = qsum[1 - zh].astype(BF16)
        swap = send(q.at[y, 1 - zh], qz, partner)
        first = jnp.sum(qsum[0] + qsum[1], axis=0, keepdims=True)
        second = jnp.sum(qsum[zh] * unit[...], axis=0, keepdims=True)
        for par, rows in ((c, nbuf[y, 1 - zh, c]), (1 - c, pbuf[...])):
            for blk in range(2):
                lo = pl.multiple_of((2 * blk + par) * rb, rb)
                second = second + jnp.sum(
                    qsum[1 - zh, pl.ds(lo, rb), :] * unit_of(rows[blk * rb:(blk + 1) * rb, :]),
                    axis=0,
                    keepdims=True,
                )
        st2[...] = jnp.zeros_like(st2)
        st2[0:1, :] = first
        st2[1:2, :] = second
        return swap, [send(st2, st2r.at[k - 1], at_y(k)) for k in range(1, NY)]

    out1 = [None] * 2

    def x_last(s):
        x_up[s].wait_recv()
        x_down[s].wait_recv()
        x1[s, x] = (
            x1[s, x].astype(F32) + xr[s, 0, rx - 1].astype(F32) + xr[s, 1, rx - 1].astype(F32)
        ).astype(BF16)
        out1[s] = [
            send(x1.at[s, x, lax.rem(z + k, NZ)], zr1.at[s, k - 1], at_z(k)) for k in range(1, NZ)
        ]

    unit[...] = unit_of(patches[...])
    other_rows.wait_recv()
    for t in range(1, max(rx, ry)):
        if t < ry:
            y_up, y_down = y_round(t)
        if t < rx:
            for s in range(2):
                x_round(s, t)
    q_swap, stats = y_last()

    x_last(0)
    for copy in z_sends:
        copy.wait_recv()
    z_sum = z1[z].astype(F32)
    for k in range(NZ - 1):
        z_sum = z_sum + zr2[k].astype(F32)
    z1[z] = z_sum.astype(BF16)
    out2 = [send(z1.at[z, lax.rem(x + k, NX)], xr2.at[k - 1], at_x(k)) for k in range(1, NX)]
    for copy in stats:
        copy.wait_recv()
    both = st2[...]
    for k in range(NY - 1):
        both = both + st2r[k]
    st3[...] = both
    stats = send(st3, st3r, partner)
    x_last(1)

    q_swap.wait_recv()
    grad_norm = qsum[zh] + qz[...].astype(F32)
    stats.wait_recv()
    both = st3[...] + st3r[...]
    first, second = both[0:1, :] * (1.0 / d_all), both[1:2, :] * (1.0 / d_all)
    result = cot[...].reshape(fb, tok).astype(F32) + inv_std * (
        grad_norm - first - unit[...] * second
    )
    out_p[...] = result.astype(BF16)

    for s in range(2):
        block = x1[s, x, z].astype(F32)
        for k, copy in enumerate(out1[s]):
            copy.wait_recv()
            block = block + zr1[s, k].astype(F32)
        out_u[:, s * cb:(s + 1) * cb] = block * scale

    block = z1[z, x].astype(F32)
    for k, copy in enumerate(out2):
        copy.wait_recv()
        block = block + xr2[k].astype(F32)
    out_u[:, 2 * cb:3 * cb] = block * scale

    for copy in started:
        copy.wait_send()


def per_device(patches, pre_act, cotangent, w_up, w_down):
    tok, fb = patches.shape
    hid = pre_act.shape[1]
    d_all = w_up.shape[0]
    rb, cb = fb // 4, hid // 3
    rx, ry = NX // 2, NY // 2
    vmem = pl.BlockSpec(memory_space=pltpu.VMEM)
    anywhere = pl.BlockSpec(memory_space=pltpu.HBM)
    grad_t, grad_up = pl.pallas_call(
        kernel,
        out_shape=(
            jax.ShapeDtypeStruct((fb, tok), BF16),
            jax.ShapeDtypeStruct((rb, hid), F32),
        ),
        in_specs=[vmem, anywhere, vmem, anywhere, anywhere],
        out_specs=(vmem, vmem),
        scratch_shapes=[
            pltpu.VMEM((d_all, hid), BF16),
            pltpu.VMEM((hid, d_all), BF16),
            pltpu.VMEM((tok, hid), BF16),
            pltpu.VMEM((NY, 2, 2, fb // 2, tok), BF16),
            pltpu.VMEM((NY, 2, 2, fb // 2, tok), BF16),
            pltpu.VMEM((2, fb // 2, tok), BF16),
            pltpu.VMEM((fb // 2, tok), BF16),
            pltpu.VMEM((hid, tok), F32),
            pltpu.VMEM((hid, tok), F32),
            pltpu.VMEM((2, tok, hid), BF16),
            pltpu.VMEM((fb, tok), F32),
            pltpu.VMEM((NY, 2, fb, tok), BF16),
            pltpu.VMEM((2, ry, 2, fb, tok), BF16),
            pltpu.VMEM((fb, tok), BF16),
            pltpu.VMEM((2, fb, tok), F32),
            pltpu.VMEM((2, NX, NZ, rb, cb), BF16),
            pltpu.VMEM((2, 2, rx, NZ, rb, cb), BF16),
            pltpu.VMEM((2, NZ - 1, rb, cb), BF16),
            pltpu.VMEM((NZ, NX, rb, cb), BF16),
            pltpu.VMEM((NZ - 1, NX, rb, cb), BF16),
            pltpu.VMEM((NX - 1, rb, cb), BF16),
            pltpu.VMEM((NY, 8, tok), F32),
            pltpu.VMEM((8, tok), F32),
            pltpu.VMEM((8, tok), F32),
            pltpu.VMEM((8, tok), F32),
            pltpu.VMEM((NY - 1, 8, tok), F32),
            pltpu.VMEM((8, tok), F32),
            pltpu.VMEM((8, tok), F32),
            pltpu.SemaphoreType.DMA((N_SEMS,)),
            pltpu.SemaphoreType.DMA((N_SEMS,)),
            pltpu.SemaphoreType.DMA((9,)),
        ],
        compiler_params=pltpu.CompilerParams(
            collective_id=0, has_side_effects=True, vmem_limit_bytes=62 * 1024 * 1024
        ),
        cost_estimate=pl.CostEstimate(
            flops=6 * tok * d_all * hid, bytes_accessed=4 * d_all * hid, transcendentals=2 * tok * hid
        ),
    )(patches.T, pre_act, cotangent.T.reshape(2, fb // 2, tok), w_up, w_down)
    return grad_t.T, grad_up


def solution(mesh):
    return jax.shard_map(
        per_device,
        mesh=mesh,
        in_specs=(P("dp", "mp"), P("dp", "mp"), P("dp", "mp"), P(None, "mp"), P("mp", None)),
        out_specs=(P("dp", "mp"), P("dp", "mp")),
        check_vma=False,
    )
```

```python
import math

import jax
import jax.numpy as jnp
from jax import lax
from jax.experimental import pallas as pl
from jax.experimental.pallas import tpu as pltpu
from jax.sharding import PartitionSpec as P

MESH = pl.DeviceIdType.MESH
F32 = jnp.float32
BF16 = jnp.bfloat16

NX, NY, NZ = 8, 8, 4


def gelu_slope(value):
    cdf_part = 0.5 * (1.0 + lax.erf(value * (1.0 / math.sqrt(2.0))))
    density = jnp.exp(-0.5 * value * value) * (1.0 / math.sqrt(2.0 * math.pi))
    return cdf_part + value * density


def add_bf16(a, b):
    return (a.astype(F32) + b.astype(F32)).astype(BF16)


class Counter:
    def __init__(self):
        self.n = 0

    def take(self):
        self.n += 1
        return self.n - 1


N_SEMS = 144


def kernel(
    patches, pre_hbm, cot, wu_hbm, wd_hbm, out_p, out_u,
    wu, wd, pre_act, cbuf, nbuf, pats, pbuf, slope, acc, gp, unit, q, qr, qz, qsum,
    x1, xr, zr1, z1, zr2, xr2, lnp, st1, st1r, st2, st2r, st3, st3r,
    ssem, rsem, wsem,
):
    fb, tok = patches.shape
    d_all = fb * 2 * NY
    rb = fb // 4
    hid = pre_act.shape[1]
    cb = hid // 3
    scale = 1.0 / math.sqrt(tok * NX * NZ * 2)
    ry, rx = NY // 2, NX // 2

    dp, mp = lax.axis_index("dp"), lax.axis_index("mp")
    c = lax.rem(dp, 2)
    x = lax.rem(dp // 2, NX)
    z = dp // (2 * NX)
    y, zh = mp // 2, lax.rem(mp, 2)

    def at_y(off):
        return {"mp": lax.rem(y + off + NY, NY) * 2 + zh}

    def at_x(off):
        return {"dp": (z * NX + lax.rem(x + off + NX, NX)) * 2 + c}

    def at_z(off):
        return {"dp": (lax.rem(z + off, NZ) * NX + x) * 2 + c}

    partner = {"mp": y * 2 + 1 - zh}
    sibling = {"dp": dp + 1 - 2 * c}

    barrier = pltpu.get_barrier_semaphore()
    greeted = (
        [at_y(k) for k in range(1, NY)]
        + [at_x(k) for k in range(1, NX)]
        + [at_z(k) for k in range(1, NZ)]
        + [sibling, partner]
    )
    for peer in greeted:
        pl.semaphore_signal(barrier, inc=1, device_id=peer, device_id_type=MESH)

    def loads(src, dst, first):
        n = src.shape[0] // 4
        return [
            pltpu.make_async_copy(
                src.at[pl.ds(i * n, n)], dst.at[pl.ds(i * n, n)], wsem.at[first + i]
            )
            for i in range(4)
        ]

    load_pre = pltpu.make_async_copy(pre_hbm, pre_act, wsem.at[8])
    load_wd, load_wu = loads(wd_hbm, wd, 0), loads(wu_hbm, wu, 4)
    for copy in [load_pre] + load_wd:
        copy.start()

    counter = Counter()
    started = []

    def send(src, dst, peer):
        i = counter.take()
        copy = pltpu.make_async_remote_copy(
            src_ref=src, dst_ref=dst, send_sem=ssem.at[i], recv_sem=rsem.at[i],
            device_id=peer, device_id_type=MESH,
        )
        copy.start()
        started.append(copy)
        return copy

    def ag_start(buf, h, t, own=None):
        up, down = lax.rem(y - t + NY, NY), lax.rem(y + t, NY)
        if t < ry - 1:
            a, b = buf.at[up, h], buf.at[down, h]
        else:
            a, b = buf.at[up, h, 0], buf.at[down, h, 1]
        if own is None:
            return send(a, a, at_y(1)), send(b, b, at_y(-1))
        if t < ry - 1:
            return send(own, a, at_y(1)), send(own, b, at_y(-1))
        return send(own.at[0], a, at_y(1)), send(own.at[1], b, at_y(-1))

    for par in range(2):
        for blk in range(2):
            lo = (2 * blk + par) * rb
            pats[par, blk * rb:(blk + 1) * rb, :] = patches[lo:lo + rb, :]

    pl.semaphore_wait(barrier, len(greeted))

    cot_swap = send(cot, cbuf.at[y, zh], partner)
    core_swap = send(pats.at[1 - c], nbuf.at[y, zh, c], sibling)
    cot_a = ag_start(cbuf, zh, 0, cot)
    pat_swap = [send(pats.at[c], nbuf.at[y, zh, c], partner)]
    nbuf[y, zh, c] = pats[c]

    cbuf[y, zh] = cot[...]
    step = 128

    def slopes(lo, hi):
        for i in range(lo, hi):
            part = jnp.transpose(pre_act[:, i * step:(i + 1) * step].astype(F32))
            slope[i * step:(i + 1) * step, :] = gelu_slope(part)

    def act_part(yp, first=False):
        lanes = pl.ds(pl.multiple_of(yp * (2 * fb), 128), 2 * fb)
        part = jnp.dot(wd[:, lanes], cbuf[yp].reshape(2 * fb, tok), preferred_element_type=F32)
        acc[...] = part if first else acc[...] + part

    def act_round(t):
        if t < ry - 1:
            act_part(lax.rem(y - 1 - t + NY, NY))
            act_part(lax.rem(y + 1 + t, NY))
        else:
            act_part(lax.rem(y + ry, NY))

    def pass_on(buf, h, copies, t):
        for copy in copies:
            copy.wait_recv()
        return None if t == ry - 1 else ag_start(buf, h, t + 1)

    def norm_part(yp):
        for k in range(2):
            block = nbuf[yp, :, k].reshape(fb, tok).astype(F32)
            total = jnp.sum(block, axis=0, keepdims=True)
            off = block - total * (1.0 / fb)
            lnp[yp, k:k + 1, :] = total
            lnp[yp, 2 + k:3 + k, :] = jnp.sum(off * off, axis=0, keepdims=True)

    def norm_round(t):
        if t < ry - 1:
            norm_part(lax.rem(y - 1 - t + NY, NY))
            norm_part(lax.rem(y + 1 + t, NY))
        else:
            norm_part(lax.rem(y + ry, NY))

    core_swap.wait_recv()
    pat_swap.append(send(nbuf.at[y, zh, 1 - c], nbuf.at[y, zh, 1 - c], partner))
    pat_a = ag_start(nbuf, zh, 0)
    load_pre.wait()
    slopes(0, hid // step)
    for t in range(ry + 1):
        if t < ry:
            cot_a = pass_on(cbuf, zh, cot_a, t)
            pat_a = pass_on(nbuf, zh, pat_a, t)
        if t == 0:
            cot_swap.wait_recv()
            cot_b = ag_start(cbuf, 1 - zh, 0)
            for copy in pat_swap:
                copy.wait_recv()
            pat_b = ag_start(nbuf, 1 - zh, 0)
            other_rows = send(nbuf.at[y, 1 - zh, 1 - c], pbuf, sibling)
            norm_part(y)
        else:
            cot_b = pass_on(cbuf, 1 - zh, cot_b, t - 1)
            if t < ry:
                pat_b = pass_on(nbuf, 1 - zh, pat_b, t - 1)
            if t == 1:
                for copy in load_wd:
                    copy.wait()
                for copy in load_wu:
                    copy.start()
                act_part(y, True)
            if t < ry:
                act_round(t - 1)
                norm_round(t - 1)
    act_round(ry - 1)
    own = acc[...] * slope[...]
    gp[c] = jnp.transpose(own).astype(BF16)
    gp_swap = send(gp.at[c], gp.at[c], sibling)
    own = own.astype(BF16)
    pass_on(nbuf, 1 - zh, pat_b, ry - 1)
    norm_round(ry - 1)

    def combine(parts, count):
        whole = parts[0][0]
        for sums, _ in parts[1:]:
            whole = whole + sums
        mean = whole * (1.0 / (count * len(parts)))
        square = None
        for sums, squares in parts:
            shift = sums * (1.0 / count) - mean
            term = squares + count * (shift * shift)
            square = term if square is None else square + term
        return whole, square

    here = combine([(lnp[yp, 0:2, :], lnp[yp, 2:4, :]) for yp in range(NY)], fb)
    st1[...] = jnp.zeros_like(st1)
    st1[0:2, :], st1[2:4, :] = here
    norm_swap = send(st1, st1r, sibling)

    for copy in load_wu:
        copy.wait()
    for yp in range(NY):
        part = jnp.dot(
            wu[yp * 2 * fb:(yp + 1) * 2 * fb, :], own, preferred_element_type=F32
        )
        q[yp] = part.astype(BF16).reshape(2, fb, tok)
    far = lax.rem(y + ry, NY)
    y_up = send(q.at[far, 0], qr.at[0, 0, 0], at_y(1))
    y_down = send(q.at[far, 1], qr.at[1, 0, 1], at_y(-1))

    norm_swap.wait_recv()
    whole, square = combine([here, (st1r[0:2, :], st1r[2:4, :])], d_all // 2)
    centres = whole * (1.0 / d_all)
    inv_stds = lax.rsqrt(square * (1.0 / d_all) + 1e-06)
    centre = jnp.where(c == 0, centres[0:1, :], centres[1:2, :])
    inv_std = jnp.where(c == 0, inv_stds[0:1, :], inv_stds[1:2, :])

    def up_part(yp):
        rows = [
            (nbuf[yp, :, k].reshape(fb, tok).astype(F32) - centres[k:k + 1, :])
            * inv_stds[k:k + 1, :]
            for k in range(2)
        ]
        part = jnp.dot(
            jnp.concatenate(rows, axis=1).astype(BF16),
            gp[...].reshape(2 * tok, hid),
            preferred_element_type=F32,
        ).astype(BF16)
        for m in range(4):
            zp, xp = divmod(4 * yp + m, NX)
            block = part[m * rb:(m + 1) * rb, :]
            x1[0, xp, zp] = block[:, 0:cb]
            x1[1, xp, zp] = block[:, cb:2 * cb]
            z1[zp, xp] = block[:, 2 * cb:3 * cb]

    gp_swap.wait_recv()
    for yp in range(NY):
        up_part(yp)

    gathered = len(started)
    nh = NZ // 2
    xfar = lax.rem(x + rx, NX)
    x_up, x_down = [None] * 2, [None] * 2
    z_sends = []
    for s in range(2):
        x_up[s] = send(x1.at[s, xfar, pl.ds(0, nh)], xr.at[s, 0, 0, pl.ds(0, nh)], at_x(1))
        x_down[s] = send(x1.at[s, xfar, pl.ds(nh, nh)], xr.at[s, 1, 0, pl.ds(nh, nh)], at_x(-1))
        if s == 0:
            for k in range(1, NZ):
                z_sends.append(send(z1.at[lax.rem(z + k, NZ)], zr2.at[k - 1], at_z(k)))

    def y_round(t):
        up, down = lax.rem(y + ry - t, NY), lax.rem(y - ry + t + NY, NY)
        y_up.wait_recv()
        if t == 1:
            q[up, 0] = add_bf16(q[up, 0], qr[0, 0, 0])
        else:
            q[up] = add_bf16(q[up], qr[0, t - 1])
        a = send(q.at[up], qr.at[0, t], at_y(1))
        y_down.wait_recv()
        if t == 1:
            q[down, 1] = add_bf16(q[down, 1], qr[1, 0, 1])
        else:
            q[down] = add_bf16(q[down], qr[1, t - 1])
        return a, send(q.at[down], qr.at[1, t], at_y(-1))

    def x_round(s, t):
        up, down = lax.rem(x + rx - t, NX), lax.rem(x - rx + t + NX, NX)
        x_up[s].wait_recv()
        n = nh if t == 1 else NZ
        x1[s, up, 0:n] = add_bf16(x1[s, up, 0:n], xr[s, 0, t - 1, 0:n])
        x_up[s] = send(x1.at[s, up], xr.at[s, 0, t], at_x(1))
        x_down[s].wait_recv()
        n = nh if t == 1 else 0
        x1[s, down, n:NZ] = add_bf16(x1[s, down, n:NZ], xr[s, 1, t - 1, n:NZ])
        x_down[s] = send(x1.at[s, down], xr.at[s, 1, t], at_x(-1))

    def unit_of(block):
        return (block.astype(F32) - centre) * inv_std

    def y_last():
        y_up.wait_recv()
        y_down.wait_recv()
        if ry == 1:
            qsum[0] = q[y, 0].astype(F32) + qr[0, 0, 0].astype(F32)
            qsum[1] = q[y, 1].astype(F32) + qr[1, 0, 1].astype(F32)
        else:
            qsum[...] = (
                q[y].astype(F32) + qr[0, ry - 1].astype(F32) + qr[1, ry - 1].astype(F32)
            )
        q[y, 1 - zh] = qsum[1 - zh].astype(BF16)
        swap = send(q.at[y, 1 - zh], qz, partner)
        first = jnp.sum(qsum[0] + qsum[1], axis=0, keepdims=True)
        second = jnp.sum(qsum[zh] * unit[...], axis=0, keepdims=True)
        for par, rows in ((c, nbuf[y, 1 - zh, c]), (1 - c, pbuf[...])):
            for blk in range(2):
                lo = pl.multiple_of((2 * blk + par) * rb, rb)
                second = second + jnp.sum(
                    qsum[1 - zh, pl.ds(lo, rb), :] * unit_of(rows[blk * rb:(blk + 1) * rb, :]),
                    axis=0,
                    keepdims=True,
                )
        st2[...] = jnp.zeros_like(st2)
        st2[0:1, :] = first
        st2[1:2, :] = second
        return swap, [send(st2, st2r.at[k - 1], at_y(k)) for k in range(1, NY)]

    out1 = [None] * 2

    def x_last(s):
        x_up[s].wait_recv()
        x_down[s].wait_recv()
        x1[s, x] = (
            x1[s, x].astype(F32) + xr[s, 0, rx - 1].astype(F32) + xr[s, 1, rx - 1].astype(F32)
        ).astype(BF16)
        out1[s] = [
            send(x1.at[s, x, lax.rem(z + k, NZ)], zr1.at[s, k - 1], at_z(k)) for k in range(1, NZ)
        ]

    unit[...] = unit_of(patches[...])
    other_rows.wait_recv()
    for t in range(1, max(rx, ry)):
        if t < ry:
            y_up, y_down = y_round(t)
        if t < rx:
            for s in range(2):
                x_round(s, t)
    for copy in started[:gathered]:
        copy.wait_send()
    reduced = len(started)
    q_swap, stats = y_last()

    x_last(0)
    for copy in z_sends:
        copy.wait_recv()
    z_sum = z1[z].astype(F32)
    for k in range(NZ - 1):
        z_sum = z_sum + zr2[k].astype(F32)
    z1[z] = z_sum.astype(BF16)
    out2 = [send(z1.at[z, lax.rem(x + k, NX)], xr2.at[k - 1], at_x(k)) for k in range(1, NX)]
    for copy in stats:
        copy.wait_recv()
    both = st2[...]
    for k in range(NY - 1):
        both = both + st2r[k]
    st3[...] = both
    stats = send(st3, st3r, partner)
    x_last(1)
    for copy in started[gathered:reduced]:
        copy.wait_send()

    q_swap.wait_recv()
    grad_norm = qsum[zh] + qz[...].astype(F32)
    stats.wait_recv()
    both = st3[...] + st3r[...]
    first, second = both[0:1, :] * (1.0 / d_all), both[1:2, :] * (1.0 / d_all)
    result = cot[...].reshape(fb, tok).astype(F32) + inv_std * (
        grad_norm - first - unit[...] * second
    )
    out_p[...] = result.astype(BF16)

    for s in range(2):
        block = x1[s, x, z].astype(F32)
        for k, copy in enumerate(out1[s]):
            copy.wait_recv()
            block = block + zr1[s, k].astype(F32)
        out_u[:, s * cb:(s + 1) * cb] = block * scale

    block = z1[z, x].astype(F32)
    for k, copy in enumerate(out2):
        copy.wait_recv()
        block = block + xr2[k].astype(F32)
    out_u[:, 2 * cb:3 * cb] = block * scale

    for copy in started[reduced:]:
        copy.wait_send()


def per_device(patches, pre_act, cotangent, w_up, w_down):
    tok, fb = patches.shape
    hid = pre_act.shape[1]
    d_all = w_up.shape[0]
    rb, cb = fb // 4, hid // 3
    rx, ry = NX // 2, NY // 2
    vmem = pl.BlockSpec(memory_space=pltpu.VMEM)
    anywhere = pl.BlockSpec(memory_space=pltpu.HBM)
    grad_t, grad_up = pl.pallas_call(
        kernel,
        out_shape=(
            jax.ShapeDtypeStruct((fb, tok), BF16),
            jax.ShapeDtypeStruct((rb, hid), F32),
        ),
        in_specs=[vmem, anywhere, vmem, anywhere, anywhere],
        out_specs=(vmem, vmem),
        scratch_shapes=[
            pltpu.VMEM((d_all, hid), BF16),
            pltpu.VMEM((hid, d_all), BF16),
            pltpu.VMEM((tok, hid), BF16),
            pltpu.VMEM((NY, 2, 2, fb // 2, tok), BF16),
            pltpu.VMEM((NY, 2, 2, fb // 2, tok), BF16),
            pltpu.VMEM((2, fb // 2, tok), BF16),
            pltpu.VMEM((fb // 2, tok), BF16),
            pltpu.VMEM((hid, tok), F32),
            pltpu.VMEM((hid, tok), F32),
            pltpu.VMEM((2, tok, hid), BF16),
            pltpu.VMEM((fb, tok), F32),
            pltpu.VMEM((NY, 2, fb, tok), BF16),
            pltpu.VMEM((2, ry, 2, fb, tok), BF16),
            pltpu.VMEM((fb, tok), BF16),
            pltpu.VMEM((2, fb, tok), F32),
            pltpu.VMEM((2, NX, NZ, rb, cb), BF16),
            pltpu.VMEM((2, 2, rx, NZ, rb, cb), BF16),
            pltpu.VMEM((2, NZ - 1, rb, cb), BF16),
            pltpu.VMEM((NZ, NX, rb, cb), BF16),
            pltpu.VMEM((NZ - 1, NX, rb, cb), BF16),
            pltpu.VMEM((NX - 1, rb, cb), BF16),
            pltpu.VMEM((NY, 8, tok), F32),
            pltpu.VMEM((8, tok), F32),
            pltpu.VMEM((8, tok), F32),
            pltpu.VMEM((8, tok), F32),
            pltpu.VMEM((NY - 1, 8, tok), F32),
            pltpu.VMEM((8, tok), F32),
            pltpu.VMEM((8, tok), F32),
            pltpu.SemaphoreType.DMA((N_SEMS,)),
            pltpu.SemaphoreType.DMA((N_SEMS,)),
            pltpu.SemaphoreType.DMA((9,)),
        ],
        compiler_params=pltpu.CompilerParams(
            collective_id=0, has_side_effects=True, vmem_limit_bytes=62 * 1024 * 1024
        ),
        cost_estimate=pl.CostEstimate(
            flops=6 * tok * d_all * hid, bytes_accessed=4 * d_all * hid, transcendentals=2 * tok * hid
        ),
    )(patches.T, pre_act, cotangent.T.reshape(2, fb // 2, tok), w_up, w_down)
    return grad_t.T, grad_up


def solution(mesh):
    return jax.shard_map(
        per_device,
        mesh=mesh,
        in_specs=(P("dp", "mp"), P("dp", "mp"), P("dp", "mp"), P(None, "mp"), P("mp", None)),
        out_specs=(P("dp", "mp"), P("dp", "mp")),
        check_vma=False,
    )
```
